256 devices in a mesh: segment: 4 (over y), dom: 64 (over x, z, core).
Axes of the slice: x: 4, y: 4, z: 8, core: 2. Of those that a mesh axis runs over, the one named last changes fastest.
Arguments:
- forward_held: float32 [4, 16384, 512], P('segment', 'dom'), may hold values from -6 to 6
- forward_new: float32 [16384, 512], P('dom'), may hold values from -6 to 6
- back_outputs: float32 [4, 16384, 512], P('segment', 'dom'), may hold values from -6 to 6
- back_cotangents: float32 [4, 16384, 512], P('segment', 'dom'), may hold values from -6 to 6
- back_new_outputs: float32 [16384, 512], P('dom'), may hold values from -6 to 6
- back_new_cotangents: float32 [16384, 512], P('dom'), may hold values from -6 to 6
- adj_tiles: float32 [128, 16, 128, 128], P('dom'), may hold values from 0 to 0.046875, as said below
- tile_cols: int32 [128, 16], P('dom'), may hold values from 0 to 127, as said below
- weight_first: float32 [8, 256, 256], P('segment'), may hold values from -0.375 to 0.375
- weight_second: float32 [8, 256, 256], P('segment'), may hold values from -0.375 to 0.375
- gain_first: float32 [8, 256], P('segment'), may hold values from 0.1 to 1.9
- gain_second: float32 [8, 256], P('segment'), may hold values from 0.1 to 1.9
Outputs:
- forward_one: float32 [4, 16384, 512], P('segment', 'dom')
- forward_two: float32 [4, 16384, 512], P('segment', 'dom')
- inputs_one: float32 [4, 16384, 512], P('segment', 'dom')
- cotan_one: float32 [4, 16384, 512], P('segment', 'dom')
- inputs_two: float32 [4, 16384, 512], P('segment', 'dom')
- cotan_two: float32 [4, 16384, 512], P('segment', 'dom')
- grad_weight_first: float32 [8, 256, 256], P('segment')
- grad_weight_second: float32 [8, 256, 256], P('segment')
- grad_gain_first: float32 [8, 256], P('segment')
- grad_gain_second: float32 [8, 256], P('segment')
The draws below stay inside these ranges and needn't reach their ends.
Inputs may be any that keep to these rules, and one draw needn't show every extreme that they name: tile_cols[r, t] lies between max(0, (r // 2 - 1) * 2) and min(128, (r // 2 + 2) * 2) - 1: a block of the row block's own partition or of the partition on either side; a column block may appear several times in a row. `adj_tiles`: each entry is zero or positive; a node's row over its 16 tiles holds about 32 nonzero entries, and its expected sum is one.
All inputs are finite; a program needn't handle non-finite values.
Results may differ from the reference program's by a relative error of at most 0.00085.
Values sent between devices are 32-bit elements; how exact they have to be, the bound alone decides.
No kernel may reach another device: no remote copies, remote signals or barrier semaphores. Data moves between devices by JAX's collectives and lax.ppermute only.
A program may use at most 128 MiB of HBM per device.

```python
import math
import jax
import jax.numpy as jnp
from jax import lax

HALF = 256
WIDTH = 512
BLOCK = 128
TILES = 16
LAY_DEV = 2
ROWB_DEV = 2
NBLK = 128
NODES = 16384
LAYERS = 8
N_SEGMENT = 4
N_DOM = 64


def draw_tile_cols(key, part):
    row_index = jnp.arange(NBLK, dtype=jnp.int32)
    owner = row_index // ROWB_DEV
    lowest = jnp.maximum(owner * ROWB_DEV - ROWB_DEV, 0)
    highest = jnp.minimum(owner * ROWB_DEV + 2 * ROWB_DEV, NBLK)
    picks = jax.random.randint(key, (NBLK, TILES), 0, 1 << 20, dtype=jnp.int32)
    return (lowest[:, None] + picks % (highest - lowest)[:, None]).astype(jnp.int32)


def draw_adj_tiles(key, part):
    row_len = TILES * BLOCK
    kept = min(row_len, 32)
    chance = kept / row_len
    key_mask = jax.random.fold_in(key, 7101)
    key_value = jax.random.fold_in(key, 7202)
    shape = (NBLK, TILES, BLOCK, BLOCK)
    mask = (jax.random.uniform(key_mask, shape, jnp.float32) < chance).astype(jnp.float32)
    values = jax.random.uniform(key_value, shape, jnp.float32, 0.5, 1.5)
    return (mask * values / kept).astype(jnp.float32)


def level_of(stream_key, extent, shards, low, largest):
    factor_of, own = 1.0, jax.random.fold_in(stream_key, 6)
    for position, parts in shards:
        draws = jnp.exp(jax.random.uniform(jax.random.fold_in(own, position), (parts,), jnp.float32, low / len(shards), largest / len(shards)))
        factor_of = factor_of * jnp.repeat(draws, extent[position] // parts).reshape([-1 if axis == position else 1 for axis in range(len(extent))])
    return factor_of


def bell_draw(own_key, shape, width, limit, pieces=(), held_as=jnp.bfloat16):
    array = jax.random.normal(own_key, shape, jnp.float32) * width
    if len(pieces) > 0:
        array = level_of(own_key, shape, pieces, -0.22, 0.18) * array
    return jnp.clip(array, min=-limit, max=limit).astype(held_as)


def setup_inputs(seed: int = 0) -> dict:
    keys = jax.random.split(jax.random.key(seed), 13)
    forward_held = bell_draw(keys[0], (N_SEGMENT, NODES, WIDTH), 1.0, 6.0, ((0, 4), (1, 64)), jnp.float32)
    forward_new = bell_draw(keys[1], (NODES, WIDTH), 1.0, 6.0, ((0, 64),), jnp.float32)
    back_outputs = bell_draw(keys[2], (N_SEGMENT, NODES, WIDTH), 1.0, 6.0, ((0, 4), (1, 64)), jnp.float32)
    back_cotangents = bell_draw(keys[3], (N_SEGMENT, NODES, WIDTH), 1.0, 6.0, ((0, 4), (1, 64)), jnp.float32)
    back_new_outputs = bell_draw(keys[4], (NODES, WIDTH), 1.0, 6.0, ((0, 64),), jnp.float32)
    back_new_cotangents = bell_draw(keys[5], (NODES, WIDTH), 1.0, 6.0, ((0, 64),), jnp.float32)
    adj_tiles = draw_adj_tiles(jax.random.fold_in(keys[12], 71), 0)
    tile_cols = draw_tile_cols(jax.random.fold_in(keys[12], 71), 0)
    weight_first = bell_draw(keys[8], (LAYERS, HALF, HALF), HALF ** -0.5, 0.375, ((0, 4),), jnp.float32)
    weight_second = bell_draw(keys[9], (LAYERS, HALF, HALF), HALF ** -0.5, 0.375, ((0, 4),), jnp.float32)
    gain_first = jnp.clip(1.0 + 0.18 * jax.random.normal(keys[10], (LAYERS, HALF), jnp.float32), 0.1, 1.9)
    gain_second = jnp.clip(1.0 + 0.18 * jax.random.normal(keys[11], (LAYERS, HALF), jnp.float32), 0.1, 1.9)
    return {"forward_held": forward_held, "forward_new": forward_new, "back_outputs": back_outputs, "back_cotangents": back_cotangents, "back_new_outputs": back_new_outputs, "back_new_cotangents": back_new_cotangents, "adj_tiles": adj_tiles, "tile_cols": tile_cols, "weight_first": weight_first, "weight_second": weight_second, "gain_first": gain_first, "gain_second": gain_second}


PRECISE = lax.Precision.HIGHEST

def prepare(node_rows, gain_vec, weight):
    row_mean = lax.optimization_barrier(jnp.mean(node_rows, axis=1, keepdims=True))
    centred = node_rows - row_mean
    spread = lax.optimization_barrier(jnp.mean(centred * centred, axis=1, keepdims=True))
    normed = centred * lax.rsqrt(spread + 1e-05) * gain_vec
    return jnp.dot(jax.nn.relu(normed), weight, precision=PRECISE)

def window_matrix(adj_tiles, tile_cols, first_block):
    row_blocks = adj_tiles.shape[0]
    block_size = adj_tiles.shape[2]
    places = jnp.arange(3 * row_blocks, dtype=jnp.int32)
    onehot = (tile_cols[:, :, None] - first_block == places[None, None, :]).astype(jnp.float32)
    banded = jnp.einsum('rtw,rtij->riwj', onehot, adj_tiles, precision=PRECISE)
    return banded.reshape(row_blocks * block_size, 3 * row_blocks * block_size)

def reference(forward_held, forward_new, back_outputs, back_cotangents, back_new_outputs, back_new_cotangents, adj_tiles, tile_cols, weight_first, weight_second, gain_first, gain_second):
    shard_rows = ROWB_DEV * BLOCK
    tiles_split = adj_tiles.reshape(N_DOM, ROWB_DEV, TILES, BLOCK, BLOCK)
    cols_split = tile_cols.reshape(N_DOM, ROWB_DEV, TILES).astype(jnp.int32)
    firsts = ((jnp.arange(N_DOM, dtype=jnp.int32) - 1) * ROWB_DEV).astype(jnp.int32)
    band_rows = jax.vmap(window_matrix)(tiles_split, cols_split, firsts)
    zeros_one = jnp.zeros((1, shard_rows, HALF), jnp.float32)

    def aggregate(values):
        blocks = values.reshape(N_DOM, shard_rows, HALF)
        padded = jnp.concatenate([zeros_one, blocks, zeros_one], axis=0)
        windows = jnp.concatenate([padded[:-2], padded[1:-1], padded[2:]], axis=1)
        return jnp.einsum('dnm,dmf->dnf', band_rows, windows, precision=PRECISE).reshape(NODES, HALF)

    def transpose_aggregate(values):
        blocks = values.reshape(N_DOM, shard_rows, HALF)
        contrib = jnp.einsum('dnm,dnf->dmf', band_rows, blocks, precision=PRECISE)
        upper = contrib[:, :shard_rows]
        middle = contrib[:, shard_rows:2 * shard_rows]
        lower = contrib[:, 2 * shard_rows:]
        total = middle + jnp.concatenate([upper[1:], zeros_one], axis=0) + jnp.concatenate([zeros_one, lower[:-1]], axis=0)
        return total.reshape(NODES, HALF)

    def forward_section(section, activations):
        for depth_idx in range(LAY_DEV):
            layer_idx = section * LAY_DEV + depth_idx
            first_half = activations[:, :HALF]
            second_half = activations[:, HALF:]
            first_half = first_half + aggregate(prepare(second_half, gain_first[layer_idx], weight_first[layer_idx]))
            second_half = second_half + aggregate(prepare(first_half, gain_second[layer_idx], weight_second[layer_idx]))
            activations = jnp.concatenate([first_half, second_half], axis=1)
        return activations
    grads_wf = [jnp.zeros((HALF, HALF), jnp.float32) for layer_idx in range(LAYERS)]
    grads_ws = [jnp.zeros((HALF, HALF), jnp.float32) for layer_idx in range(LAYERS)]
    grads_gf = [jnp.zeros((HALF,), jnp.float32) for layer_idx in range(LAYERS)]
    grads_gs = [jnp.zeros((HALF,), jnp.float32) for layer_idx in range(LAYERS)]

    def backward_section(section, outputs, cotangents):
        for depth_idx in reversed(range(LAY_DEV)):
            layer_idx = section * LAY_DEV + depth_idx
            upper_out = outputs[:, :HALF]
            lower_out = outputs[:, HALF:]
            upper_cot = cotangents[:, :HALF]
            lower_cot = cotangents[:, HALF:]
            mixed_second, pull_second = jax.vjp(prepare, upper_out, gain_second[layer_idx], weight_second[layer_idx])
            lower_in = lower_out - aggregate(mixed_second)
            extra_upper, dgain_second, dweight_second = pull_second(transpose_aggregate(lower_cot))
            carried = upper_cot + extra_upper
            mixed_first, pull_first = jax.vjp(prepare, lower_in, gain_first[layer_idx], weight_first[layer_idx])
            upper_in = upper_out - aggregate(mixed_first)
            extra_lower, dgain_first, dweight_first = pull_first(transpose_aggregate(carried))
            outputs = jnp.concatenate([upper_in, lower_in], axis=1)
            cotangents = jnp.concatenate([carried, lower_cot + extra_lower], axis=1)
            grads_wf[layer_idx] = grads_wf[layer_idx] + dweight_first
            grads_ws[layer_idx] = grads_ws[layer_idx] + dweight_second
            grads_gf[layer_idx] = grads_gf[layer_idx] + dgain_first
            grads_gs[layer_idx] = grads_gs[layer_idx] + dgain_second
        return (outputs, cotangents)
    forward_one = [forward_section(section, forward_held[section]) for section in range(N_SEGMENT)]
    entries = [forward_new] + forward_one[:-1]
    forward_two = [forward_section(section, entries[section]) for section in range(N_SEGMENT)]
    results_one = [backward_section(section, back_outputs[section], back_cotangents[section]) for section in range(N_SEGMENT)]
    results_two = []
    for section in range(N_SEGMENT):
        if section == N_SEGMENT - 1:
            results_two.append(backward_section(section, back_new_outputs, back_new_cotangents))
        else:
            results_two.append(backward_section(section, results_one[section + 1][0], results_one[section + 1][1]))
    scale_factor = 1.0 / math.sqrt(2.0 * NODES)
    return (jnp.stack(forward_one), jnp.stack(forward_two), jnp.stack([pair_item[0] for pair_item in results_one]), jnp.stack([pair_item[1] for pair_item in results_one]), jnp.stack([pair_item[0] for pair_item in results_two]), jnp.stack([pair_item[1] for pair_item in results_two]), jnp.stack(grads_wf) * scale_factor, jnp.stack(grads_ws) * scale_factor, jnp.stack(grads_gf) * scale_factor, jnp.stack(grads_gs) * scale_factor)
```

```python
import functools
import math

import jax
import jax.numpy as jnp
from jax import lax
from jax.experimental import pallas as pl
from jax.experimental.pallas import tpu as pltpu
from jax.sharding import PartitionSpec as P

F32 = jnp.float32
BF16 = jnp.bfloat16
N = 256
BLOCK = 128
TILES = 16
ORDER = "iififififfiififififf"


def split(x):
    hi = x.astype(BF16)
    lo = (x - hi.astype(F32)).astype(BF16)
    return hi, lo


def mm(a, b):
    return jnp.dot(a, b, preferred_element_type=F32)


def dot3(ah, al, bh, bl):
    return mm(ah, bh) + (mm(ah, bl) + mm(al, bh))


def norm(h):
    centred = h - jnp.mean(h, axis=1, keepdims=True)
    rstd = lax.rsqrt(jnp.mean(centred * centred, axis=1, keepdims=True) + 1e-05)
    return centred * rstd, rstd


def dot6(a, b):
    return jnp.dot(a, b, precision=lax.Precision.HIGHEST, preferred_element_type=F32)


def prepared(exact, h, gain, weight):
    xhat, _ = norm(h)
    act = jnp.maximum(xhat * gain, 0.0)
    return dot6(act, weight) if exact else dot3(*split(act), *split(weight))


def half(array, j):
    return array, pl.BlockSpec((N, N), lambda i: (0, j))


def layer(array, l):
    return array, pl.BlockSpec((None, N, N), lambda i: (l, 0, 0))


def run(kernel, outs, *operands, flops=0, scratch=()):
    arrays, specs = [], []
    for o in operands:
        if isinstance(o, tuple):
            arrays.append(o[0])
            specs.append(o[1])
        else:
            arrays.append(o)
            specs.append(pl.BlockSpec(memory_space=pltpu.VMEM))
    shapes = [jax.ShapeDtypeStruct(s, t) for s, t in outs]
    moved = sum(math.prod(s) * jnp.dtype(t).itemsize for s, t in outs) + N * N * 4 * len(arrays)
    result = pl.pallas_call(
        kernel,
        out_shape=shapes,
        grid=(1,),
        in_specs=specs,
        out_specs=[pl.BlockSpec(memory_space=pltpu.VMEM)] * len(outs),
        scratch_shapes=list(scratch),
        compiler_params=pltpu.CompilerParams(vmem_limit_bytes=12 << 20),
        cost_estimate=pl.CostEstimate(flops=flops, bytes_accessed=moved, transcendentals=0),
    )(*arrays)
    return result


MAT = ((N, N), F32)
PRODUCT = 6 * N * N * N


def band_kernel(
    tiles, cols, own, edge, own_h, own_l, edge_h, edge_l, tfar_h, tfar_l, tnear_h, tnear_l, acc
):
    dom = lax.axis_index("dom")
    parity = lax.rem(dom, 2)
    first = (dom - 1) * 2
    acc[...] = jnp.zeros_like(acc)
    for r in range(2):
        for t in range(TILES):
            place = cols[r, t] - first
            group = place // 2
            side = jnp.where(group == 2, 1, 0)
            which = jnp.where(group == 1, 0, jnp.where(side == parity, 2, 1))
            slot = r * 6 + which * 2 + (place - group * 2)
            acc[slot] += tiles[r, t]
    for r in range(2):
        rows = slice(r * BLOCK, (r + 1) * BLOCK)
        for c in range(6):
            block = acc[r * 6 + c]
            hi, lo = split(block)
            if c < 2:
                columns = slice(c * BLOCK, (c + 1) * BLOCK)
                own[rows, columns] = block
                own_h[rows, columns] = hi
                own_l[rows, columns] = lo
            else:
                columns = slice((c - 2) * BLOCK, (c - 1) * BLOCK)
                edge[rows, columns] = block
                edge_h[rows, columns] = hi
                edge_l[rows, columns] = lo
            thi, tlo = split(block.T)
            if c < 4:
                place = slice(c * BLOCK, (c + 1) * BLOCK)
                tnear_h[place, rows] = thi
                tnear_l[place, rows] = tlo
            else:
                place = slice((c - 4) * BLOCK, (c - 3) * BLOCK)
                tfar_h[place, rows] = thi
                tfar_l[place, rows] = tlo


def band_blocks(adj_tiles, tile_cols):
    return run(
        band_kernel,
        [
            MAT,
            ((N, 2 * N), F32),
            ((N, N), BF16),
            ((N, N), BF16),
            ((N, 2 * N), BF16),
            ((N, 2 * N), BF16),
            ((N, N), BF16),
            ((N, N), BF16),
            ((2 * N, N), BF16),
            ((2 * N, N), BF16),
        ],
        adj_tiles,
        (tile_cols, pl.BlockSpec(memory_space=pltpu.SMEM)),
        scratch=[pltpu.VMEM((12, BLOCK, BLOCK), F32)],
        flops=PRODUCT,
    )


TOP, LOW = slice(0, N), slice(N, 2 * N)
TOKEN = ((8, 128), F32)
PACK = ((2 * N, N), F32)
FULL = ((N, 2 * N), F32)


def aggregate3(blocks, columns, values):
    return dot3(blocks[0][:, columns], blocks[1][:, columns], *split(values))


def owed_to(blocks, g):
    return dot3(blocks[0][...], blocks[1][...], *split(g))


def pulled(l, h, back, target, gain, weight):
    scale = gain[l : l + 1, :]
    xhat, rstd = norm(h)
    grown = dot3(*split(back), *split(weight[...].T))
    dxhat = jnp.where(xhat * scale > 0.0, grown, 0.0) * scale
    inner = jnp.mean(dxhat * xhat, axis=1, keepdims=True)
    return target + rstd * (dxhat - jnp.mean(dxhat, axis=1, keepdims=True) - xhat * inner)


def weight_grad(l, h, back, gain):
    xhat, _ = norm(h)
    act = jnp.maximum(xhat * gain[l : l + 1, :], 0.0)
    return dot3(*split(act.T), *split(back))


def forward_entry_kernel(x2, gain, weight, token_in, mixed, token):
    mixed[...] = prepared(False, x2[...], gain[0:1, :], weight[...])
    token[...] = token_in[...]


def forward_next_kernel(x_new, low_moved, top_moved, gain, weight, token_in, x1, x2, mixed, token):
    use_new = lax.axis_index("segment") == 0
    value = jnp.where(use_new, x_new[:, LOW], low_moved[...])
    x1[...] = jnp.where(use_new, x_new[:, TOP], top_moved[...])
    x2[...] = value
    mixed[...] = prepared(False, value, gain[0:1, :], weight[...])
    token[...] = token_in[...]


def forward_local_kernel(target, mixed, own_h, own_l, token_in, partial, again, token):
    m = mixed[...]
    again[...] = m
    partial[...] = target[...] + aggregate3((own_h, own_l), TOP, m)
    token[...] = token_in[...]


def forward_sum(partial, near, far, edge_h, edge_l):
    edge = (edge_h, edge_l)
    return partial[...] + (aggregate3(edge, TOP, near[...]) + aggregate3(edge, LOW, far[...]))


def forward_join_kernel(
    l, partial, near, far, edge_h, edge_l, gain, weight, token_in, out, mixed, token
):
    value = forward_sum(partial, near, far, edge_h, edge_l)
    out[...] = value
    mixed[...] = prepared(False, value, gain[l : l + 1, :], weight[...])
    token[...] = token_in[...]


def forward_last_kernel(partial, near, far, edge_h, edge_l, top, token_in, whole, low, token):
    value = forward_sum(partial, near, far, edge_h, edge_l)
    whole[:, TOP] = top[...]
    whole[:, LOW] = value
    low[...] = value
    token[...] = token_in[...]


def inverse_entry_kernel(l, y1, g2, tfar_h, tfar_l, gain, weight, sent, token):
    sent[TOP, :] = prepared(True, y1[...], gain[l : l + 1, :], weight[...])
    sent[LOW, :] = owed_to((tfar_h, tfar_l), g2[...])
    token[...] = jnp.zeros_like(token)


def inverse_next_kernel(
    l, at, y_new, g_new, early, late, tfar_h, tfar_l, gain, weight, token_in,
    y1, y2, g1, g2, sent, token,
):
    use_new = lax.axis_index("segment") == at
    first = jnp.where(use_new, y_new[:, TOP], late[TOP, :])
    second = jnp.where(use_new, g_new[:, LOW], late[LOW, :])
    sent[TOP, :] = prepared(True, first, gain[l : l + 1, :], weight[...])
    sent[LOW, :] = owed_to((tfar_h, tfar_l), second)
    y1[...] = first
    g2[...] = second
    y2[...] = jnp.where(use_new, y_new[:, LOW], early[TOP, :])
    g1[...] = jnp.where(use_new, g_new[:, TOP], early[LOW, :])
    token[...] = token_in[...]


def inverse_local_kernel(grad_l, has_before, target, sent, g, own, tnear_h, tnear_l, token_in, *refs):
    partial, owed, sib, token = refs[-5:-1] if grad_l is not None else refs[-4:]
    m = sent[TOP, :]
    both = owed_to((tnear_h, tnear_l), g[...])
    sib[TOP, :] = m
    sib[LOW, :] = both[LOW]
    owed[...] = both[TOP]
    partial[...] = target[...] - dot6(own[...], m)
    if grad_l is not None:
        h, back, gain = refs[:3]
        value = weight_grad(grad_l, h[...], back[...], gain)
        refs[-1][...] = refs[3][...] + value if has_before else value
    token[...] = token_in[...]


def inverse_sums(partial, owed, near, far, edge):
    total = dot6(edge[:, TOP], near[TOP, :]) + dot6(edge[:, LOW], far[TOP, :])
    return partial[...] - total, owed[...] + near[LOW, :] + far[LOW, :]


def inverse_join_kernel(
    l, next_l, partial, owed, near, far, edge, h, cot, gain, weight, next_gain, next_weight,
    tfar_h, tfar_l, token_in, out, out_cot, back, sent, token, *packed,
):
    value, sums = inverse_sums(partial, owed, near, far, edge)
    sent[TOP, :] = prepared(True, value, next_gain[next_l : next_l + 1, :], next_weight[...])
    carried = pulled(l, h[...], sums, cot[...], gain, weight)
    sent[LOW, :] = owed_to((tfar_h, tfar_l), carried)
    out[...] = value
    out_cot[...] = carried
    back[...] = sums
    if packed:
        packed[0][TOP, :] = value
        packed[0][LOW, :] = carried
    token[...] = token_in[...]


def inverse_last_kernel(
    l, final, partial, owed, near, far, edge, h, cot, gain, weight, low, top_cot, token_in, *refs
):
    whole, whole_cot, token = refs[-5:-2]
    value, sums = inverse_sums(partial, owed, near, far, edge)
    carried = pulled(l, h[...], sums, cot[...], gain, weight)
    whole[:, TOP] = value
    whole[:, LOW] = low[...]
    whole_cot[:, TOP] = top_cot[...]
    whole_cot[:, LOW] = carried
    token[...] = token_in[...]
    if not final:
        back, packed = refs[-2:]
        back[...] = sums
        packed[TOP, :] = value
        packed[LOW, :] = carried
    else:
        first_before, first_high, second_low, second_high = refs[:4]
        keep, give = refs[-2:]
        grad = first_before[...] + weight_grad(l, h[...], sums, gain)
        even = lax.rem(lax.axis_index("dom"), 2) == 0
        keep[TOP, :] = jnp.where(even, grad, second_low[...])
        keep[LOW, :] = jnp.where(even, first_high[...], second_high[...])
        give[TOP, :] = jnp.where(even, second_low[...], grad)
        give[LOW, :] = jnp.where(even, second_high[...], first_high[...])


def add_kernel(a, b, out):
    out[...] = a[...] + b[...]


def share_kernel(scale, parts, out):
    total = jnp.sum(parts[...], axis=0) * scale
    out[...] = jnp.broadcast_to(total[None], out.shape)


def finish_kernel(
    mine, theirs, weight_first, weight_second, gain_first, gain_second, first, second, dgf, dgs
):
    even = lax.rem(lax.axis_index("dom"), 2) == 0
    a = mine[...]
    b = theirs[...]
    wf = jnp.where(even, a, b).reshape(first.shape)
    ws = jnp.where(even, b, a).reshape(second.shape)
    first[...] = wf
    second[...] = ws
    dgf[...] = jnp.sum(wf * weight_first[...], axis=2) / gain_first[...]
    dgs[...] = jnp.sum(ws * weight_second[...], axis=2) / gain_second[...]


def per_device(
    forward_held,
    forward_new,
    back_outputs,
    back_cotangents,
    back_new_outputs,
    back_new_cotangents,
    adj_tiles,
    tile_cols,
    weight_first,
    weight_second,
    gain_first,
    gain_second,
):
    dom_count = lax.axis_size("dom")
    last = lax.axis_size("segment") - 1
    layers = weight_first.shape[0]
    top = layers - 1
    up = [(i, i + 1) for i in range(1, dom_count - 1, 2)]
    far_pairs = up + [(j, i) for i, j in up]
    sib_pairs = [(i, i ^ 1) for i in range(dom_count)]
    gains = {"first": gain_first, "second": gain_second}
    weights = {"first": weight_first, "second": weight_second}

    def far(v):
        return lax.ppermute(v, "dom", far_pairs)

    def near(v):
        return lax.ppermute(v, "dom", sib_pairs)

    def onward(v):
        return lax.ppermute(v, "segment", [(i, i + 1) for i in range(last)])

    def backward(v):
        return lax.ppermute(v, "segment", [(i + 1, i) for i in range(last)])

    own_f, edge_f, own_h, own_l, edge_h, edge_l, tfar_h, tfar_l, tnear_h, tnear_l = band_blocks(
        adj_tiles, tile_cols
    )
    part = functools.partial
    token = None
    grads = {}
    results = {}

    def forward_steps():
        nonlocal token
        held = forward_held[0]
        x1, x2 = half(held, 0), half(held, 1)
        mixed, token = run(
            forward_entry_kernel, [MAT, TOKEN], x2, gain_first, layer(weight_first, 0), token,
            flops=PRODUCT,
        )
        for slot in range(2):
            for step in range(2 * layers):
                target = x1 if step % 2 == 0 else x2
                from_far = far(mixed)
                partial, again, token = run(
                    forward_local_kernel, [MAT, MAT, TOKEN], target, mixed, own_h, own_l, token,
                    flops=PRODUCT,
                )
                from_near = near(again)
                yield
                sums = (partial, from_near, from_far, edge_h, edge_l)
                if step < 2 * layers - 1:
                    name, l = ("second", step // 2) if step % 2 == 0 else ("first", step // 2 + 1)
                    value, mixed, token = run(
                        part(forward_join_kernel, l), [MAT, MAT, TOKEN], *sums, gains[name],
                        layer(weights[name], l), token, flops=3 * PRODUCT,
                    )
                    if step % 2 == 0:
                        x1 = value
                    else:
                        x2 = value
                    if step == 2 * layers - 2 and slot == 0:
                        top_moved = onward(x1)
                else:
                    whole, low, token = run(
                        forward_last_kernel, [FULL, MAT, TOKEN], *sums, x1, token, flops=2 * PRODUCT
                    )
            results["forward", slot] = whole
            if slot == 0:
                low_moved = onward(low)
                yield
                x1, x2, mixed, token = run(
                    forward_next_kernel, [MAT, MAT, MAT, TOKEN], forward_new, low_moved, top_moved,
                    gain_first, layer(weight_first, 0), token, flops=PRODUCT,
                )

    def inverse_steps():
        nonlocal token
        out, cot = back_outputs[0], back_cotangents[0]
        y1, y2, g1, g2 = half(out, 0), half(out, 1), half(cot, 0), half(cot, 1)
        sent, token = run(
            part(inverse_entry_kernel, top), [PACK, TOKEN], y1, g2, tfar_h, tfar_l, gain_second,
            layer(weight_second, top), flops=2 * PRODUCT,
        )
        pending = None
        for slot in range(2):
            for step in range(2 * layers):
                l = top - step // 2
                name = "second" if step % 2 == 0 else "first"
                target, h, g, cot = (y2, y1, g2, g1) if step % 2 == 0 else (y1, y2, g1, g2)
                from_far = far(sent)
                operands = [target, sent, g, own_f, tnear_h, tnear_l, token]
                outs = [MAT, MAT, PACK, TOKEN]
                grad_l, has_before = None, False
                if pending is not None:
                    key, point, back = pending
                    grad_l, has_before = key[1], key in grads
                    operands += [point, back, gains[key[0]]]
                    operands += [grads[key]] if has_before else []
                    outs.append(MAT)
                partial, owed, sib, token, *grad = run(
                    part(inverse_local_kernel, grad_l, has_before), outs, *operands, flops=4 * PRODUCT
                )
                if grad:
                    grads[key] = grad[0]
                from_near = near(sib)
                yield
                operands = [partial, owed, from_near, from_far, edge_f, h, cot, gains[name]]
                operands.append(layer(weights[name], l))
                if step < 2 * layers - 1:
                    following = ("first", l) if step % 2 == 0 else ("second", l - 1)
                    packed = [PACK] if slot == 0 and step == 2 * layers - 2 else []
                    value, carried, back, sent, token, *packed = run(
                        part(inverse_join_kernel, l, following[1]), [MAT, MAT, MAT, PACK, TOKEN] + packed,
                        *operands, gains[following[0]], layer(weights[following[0]], following[1]),
                        tfar_h, tfar_l, token, flops=6 * PRODUCT,
                    )
                    if packed:
                        early = backward(packed[0])
                    pending = ((name, l), h, back)
                    if step % 2 == 0:
                        y2, g1 = value, carried
                    else:
                        y1, g2 = value, carried
                elif slot == 0:
                    whole, whole_cot, token, back, packed = run(
                        part(inverse_last_kernel, l, False), [FULL, FULL, TOKEN, MAT, PACK],
                        *operands, y2, g1, token, flops=4 * PRODUCT,
                    )
                    pending = ((name, l), h, back)
                    late = backward(packed)
                else:
                    whole, whole_cot, token, keep, give = run(
                        part(inverse_last_kernel, l, True), [FULL, FULL, TOKEN, PACK, PACK],
                        *operands, y2, g1, token, grads["first", 0], grads["first", 1],
                        grads["second", 0], grads["second", 1], flops=5 * PRODUCT,
                    )
                    results["give"], results["keep"] = give, keep
            results["inputs", slot], results["cotan", slot] = whole, whole_cot
            if slot == 0:
                yield
                y1, y2, g1, g2, sent, token = run(
                    part(inverse_next_kernel, top, last), [MAT, MAT, MAT, MAT, PACK, TOKEN],
                    back_new_outputs, back_new_cotangents, early, late, tfar_h, tfar_l, gain_second,
                    layer(weight_second, top), token, flops=2 * PRODUCT,
                )

    inverse, forward = inverse_steps(), forward_steps()
    for letter in ORDER:
        next(inverse if letter == "i" else forward, None)

    theirs = near(results["give"])
    groups = [list(range(c, dom_count, 2)) for c in range(2)]
    chips = dom_count // 2
    shares = (chips, layers * N // chips, N)

    def exchanged(v):
        return lax.all_to_all(v, "dom", 0, 0, axis_index_groups=groups, tiled=True)

    summed = run(add_kernel, [PACK], results["keep"], theirs)[0]
    parts = exchanged(summed.reshape(shares))
    scale_factor = 1.0 / math.sqrt(2.0 * N * dom_count)
    mine = exchanged(run(part(share_kernel, scale_factor), [(shares, F32)], parts)[0])
    mine = mine.reshape(layers * N, N)
    square, line = ((layers, N, N), F32), ((layers, N), F32)
    finals = run(
        finish_kernel, [square, square, line, line], mine, near(mine), weight_first, weight_second,
        gain_first, gain_second,
    )
    keys = [("forward", 0), ("forward", 1), ("inputs", 0), ("cotan", 0), ("inputs", 1), ("cotan", 1)]
    return tuple(results[key][None] for key in keys) + tuple(finals)


def solution(mesh):
    rows = P("segment", "dom", None)
    nodes = P("dom", None)
    weights = P("segment", None, None)
    gains = P("segment", None)
    return jax.shard_map(
        per_device,
        mesh=mesh,
        in_specs=(
            rows,
            nodes,
            rows,
            rows,
            nodes,
            nodes,
            P("dom", None, None, None),
            nodes,
            weights,
            weights,
            gains,
            gains,
        ),
        out_specs=(rows,) * 6 + (weights, weights, gains, gains),
        check_vma=False,
    )
```

```python
import functools
import math

import jax
import jax.numpy as jnp
from jax import lax
from jax.experimental import pallas as pl
from jax.experimental.pallas import tpu as pltpu
from jax.sharding import PartitionSpec as P

F32 = jnp.float32
BF16 = jnp.bfloat16
N = 256
BLOCK = 128
TILES = 16
LAYERS = 2
FIRST, SECOND = 0, 1
A, B, C = slice(0, N), slice(N, 2 * N), slice(2 * N, 3 * N)


def split(x):
    hi = x.astype(BF16)
    return hi, (x - hi.astype(F32)).astype(BF16)


def split3(x):
    hi = x.astype(BF16)
    rest = x - hi.astype(F32)
    mid = rest.astype(BF16)
    return hi, mid, (rest - mid.astype(F32)).astype(BF16)


def mm(a, b):
    return jnp.dot(a, b, preferred_element_type=F32)


def dot3(a, b):
    return mm(a[0], b[0]) + (mm(a[0], b[1]) + mm(a[1], b[0]))


def dot6(a, b):
    small = mm(a[0], b[2]) + (mm(a[2], b[0]) + mm(a[1], b[1]))
    return mm(a[0], b[0]) + ((mm(a[0], b[1]) + mm(a[1], b[0])) + small)


def norm(h):
    centred = h - jnp.mean(h, axis=1, keepdims=True)
    rstd = lax.rsqrt(jnp.mean(centred * centred, axis=1, keepdims=True) + 1e-05)
    return centred * rstd, rstd


def active(h, gain):
    return jnp.maximum(norm(h)[0] * gain, 0.0)


def at(branch, l):
    return branch * LAYERS + l


def half(array, j):
    return array, pl.BlockSpec((N, N), lambda i: (0, j))


def run(kernel, outs, *operands, flops=0, scratch=()):
    arrays, specs = [], []
    for o in operands:
        pair = isinstance(o, tuple)
        arrays.append(o[0] if pair else o)
        specs.append(o[1] if pair else pl.BlockSpec(memory_space=pltpu.VMEM))
    return pl.pallas_call(
        kernel,
        out_shape=[jax.ShapeDtypeStruct(s, t) for s, t in outs],
        grid=(1,),
        in_specs=specs,
        out_specs=[pl.BlockSpec(memory_space=pltpu.VMEM)] * len(outs),
        scratch_shapes=list(scratch),
        compiler_params=pltpu.CompilerParams(vmem_limit_bytes=12 << 20),
        cost_estimate=pl.CostEstimate(flops=flops, bytes_accessed=1024, transcendentals=0),
    )(*arrays)


MAT = ((N, N), F32)
PAIR = ((2 * N, N), F32)
PACK = ((3 * N, N), F32)
FULL = ((N, 2 * N), F32)
THIN = ((N, BLOCK), F32)
PRODUCT = 1024


def band_kernel(tiles, cols, band, across, acc):
    dom = lax.axis_index("dom")
    parity = lax.rem(dom, 2)
    first = (dom - 1) * 2
    acc[...] = jnp.zeros_like(acc)
    for r in range(2):
        for t in range(TILES):
            place = cols[r, t] - first
            group = place // 2
            side = jnp.where(group == 2, 1, 0)
            which = jnp.where(group == 1, 0, jnp.where(side == parity, 2, 1))
            acc[r * 6 + which * 2 + (place - group * 2)] += tiles[r, t]
    for r in range(2):
        rows = slice(r * BLOCK, (r + 1) * BLOCK)
        for c in range(6):
            columns = slice(c * BLOCK, (c + 1) * BLOCK)
            block = acc[r * 6 + c]
            for i, piece in enumerate(split3(block)):
                band[i, rows, columns] = piece
            for i, piece in enumerate(split(block.T)):
                across[i, columns, rows] = piece


def weight_kernel(first, second, gain_first, gain_second, gains, weights, turned):
    for branch, (w, gain) in enumerate([(first, gain_first), (second, gain_second)]):
        for l in range(LAYERS):
            k = at(branch, l)
            gains[k : k + 1, :] = gain[l : l + 1, :]
            value = w[l]
            for i, piece in enumerate(split3(value)):
                weights[i, k] = piece
            for i, piece in enumerate(split(value.T)):
                turned[i, k] = piece


def pieces(ref, *where, count):
    return [ref[(i, *where)] for i in range(count)]


def mixed6(h, k, gains, weights):
    return dot6(split3(active(h, gains[k : k + 1, :])), pieces(weights, k, count=3))


def mixed3(h, k, gains, weights):
    return dot3(split(active(h, gains[k : k + 1, :])), pieces(weights, k, count=2))


def aggregate6(band, columns, values):
    return dot6(pieces(band, slice(0, N), columns, count=3), split3(values))


def aggregate3(band, columns, values):
    return dot3(pieces(band, slice(0, N), columns, count=2), split(values))


def owed_to(across, rows, g):
    return dot3(pieces(across, rows, slice(0, N), count=2), split(g))


def pulled(k, xhat, rstd, back, target, gains, turned):
    scale = gains[k : k + 1, :]
    grown = dot3(split(back), pieces(turned, k, count=2))
    dxhat = jnp.where(xhat * scale > 0.0, grown, 0.0) * scale
    inner = jnp.mean(dxhat * xhat, axis=1, keepdims=True)
    return target + rstd * (dxhat - jnp.mean(dxhat, axis=1, keepdims=True) - xhat * inner)


def weight_grad(k, xhat, back, gains):
    act = jnp.maximum(xhat * gains[k : k + 1, :], 0.0)
    return dot3(split(act.T), split(back))


def entry_kernel(l, y1, g2, x2, across, gain_second, weight_second, gain_first, weight_first, sent):
    act = active(y1[...], gain_second[l : l + 1, :])
    sent[A, :] = dot6(split3(act), split3(weight_second[l]))
    sent[B, :] = owed_to(across, C, g2[...])
    act = active(x2[...], gain_first[0:1, :])
    sent[C, :] = dot3(split(act), split(weight_first[0]))


def next_kernel(
    k, y_new, g_new, x_new, early, late, ahead, across, gains, weights,
    y1, y2, g1, g2, x1, x2, sent,
):
    segment = lax.axis_index("segment")
    is_last = segment == lax.axis_size("segment") - 1
    is_first = segment == 0
    upper = jnp.where(is_last, y_new[:, A], late[A, :])
    lower_cot = jnp.where(is_last, g_new[:, B], late[B, :])
    lower = jnp.where(is_first, x_new[:, B], ahead[B, :])
    sent[A, :] = mixed6(upper, k, gains, weights)
    sent[B, :] = owed_to(across, C, lower_cot)
    sent[C, :] = mixed3(lower, at(FIRST, 0), gains, weights)
    y1[...] = upper
    g2[...] = lower_cot
    x2[...] = lower
    y2[...] = jnp.where(is_last, y_new[:, B], early[A, :])
    g1[...] = jnp.where(is_last, g_new[:, A], early[B, :])
    x1[...] = jnp.where(is_first, x_new[:, A], ahead[A, :])


def local_kernel(sent, target, g, x, band, across, inverse, owed, forward, sib, sib_owed):
    mixed, fed = sent[A, :], sent[C, :]
    value = g[...]
    sib[A, :] = mixed
    sib[B, :] = fed
    sib_owed[...] = owed_to(across, B, value)
    owed[...] = owed_to(across, A, value)
    inverse[...] = target[...] - aggregate6(band, A, mixed)
    forward[...] = x[...] + aggregate3(band, A, fed)


def near_kernel(
    inverse, owed, forward, near, near_owed, h, band, inverse_out, owed_out, forward_out, xhat, rstd
):
    inverse_out[...] = inverse[...] - aggregate6(band, B, near[A, :])
    owed_out[...] = owed[...] + near_owed[...]
    forward_out[...] = forward[...] + aggregate3(band, B, near[B, :])
    normed, scale = norm(h[...])
    xhat[...] = normed
    rstd[...] = jnp.broadcast_to(scale, rstd.shape)


def joined(k, inverse, owed, forward, far, xhat, rstd, cot, band, gains, turned):
    value = inverse[...] - aggregate6(band, C, far[A, :])
    back = owed[...] + far[B, :]
    carried = pulled(k, xhat[...], rstd[:, 0:1], back, cot[...], gains, turned)
    ahead = forward[...] + aggregate3(band, C, far[C, :])
    return value, back, carried, ahead


def join_kernel(
    k, inverse_k, forward_k, inverse, owed, forward, far, xhat, rstd, cot, band, gains, turned,
    across, weights, value_out, carried_out, ahead_out, back_out, sent, *packed,
):
    value, back, carried, ahead = joined(
        k, inverse, owed, forward, far, xhat, rstd, cot, band, gains, turned
    )
    sent[A, :] = mixed6(value, inverse_k, gains, weights)
    sent[B, :] = owed_to(across, C, carried)
    sent[C, :] = mixed3(ahead, forward_k, gains, weights)
    value_out[...] = value
    carried_out[...] = carried
    ahead_out[...] = ahead
    back_out[...] = back
    if packed:
        packed[0][A, :] = value
        packed[0][B, :] = carried


def grad_kernel(k, xhat, back, gains, *refs):
    value = weight_grad(k, xhat[...], back[...], gains)
    refs[-1][...] = value + refs[0][...] if len(refs) > 1 else value


def last_kernel(
    final, k, inverse, owed, forward, far, xhat, rstd, cot, band, gains, turned, low, top_cot, top,
    *refs,
):
    if final:
        before, first_high, second_low, second_high, *refs = refs
    whole, whole_cot, whole_ahead, *refs = refs
    value, back, carried, ahead = joined(
        k, inverse, owed, forward, far, xhat, rstd, cot, band, gains, turned
    )
    whole[:, A] = value
    whole[:, B] = low[...]
    whole_cot[:, A] = top_cot[...]
    whole_cot[:, B] = carried
    whole_ahead[:, A] = top[...]
    whole_ahead[:, B] = ahead
    if final:
        keep, give = refs
        grad = before[...] + weight_grad(k, xhat[...], back, gains)
        even = lax.rem(lax.axis_index("dom"), 2) == 0
        keep[A, :] = jnp.where(even, grad, second_low[...])
        keep[B, :] = jnp.where(even, first_high[...], second_high[...])
        give[A, :] = jnp.where(even, second_low[...], grad)
        give[B, :] = jnp.where(even, second_high[...], first_high[...])
    else:
        back_out, late, ahead_out = refs
        back_out[...] = back
        late[A, :] = value
        late[B, :] = carried
        ahead_out[A, :] = top[...]
        ahead_out[B, :] = ahead


def add_kernel(a, b, out):
    out[...] = a[...] + b[...]


def share_kernel(scale, parts, out):
    total = jnp.sum(parts[...], axis=0) * scale
    out[...] = jnp.broadcast_to(total[None], out.shape)


def finish_kernel(
    mine, theirs, weight_first, weight_second, gain_first, gain_second, first, second, dgf, dgs
):
    even = lax.rem(lax.axis_index("dom"), 2) == 0
    a = mine[...]
    b = theirs[...]
    wf = jnp.where(even, a, b).reshape(first.shape)
    ws = jnp.where(even, b, a).reshape(second.shape)
    first[...] = wf
    second[...] = ws
    dgf[...] = jnp.sum(wf * weight_first[...], axis=2) / gain_first[...]
    dgs[...] = jnp.sum(ws * weight_second[...], axis=2) / gain_second[...]


def per_device(
    forward_held,
    forward_new,
    back_outputs,
    back_cotangents,
    back_new_outputs,
    back_new_cotangents,
    adj_tiles,
    tile_cols,
    weight_first,
    weight_second,
    gain_first,
    gain_second,
):
    dom_count = lax.axis_size("dom")
    last = lax.axis_size("segment") - 1
    top_layer = LAYERS - 1
    up = [(i, i + 1) for i in range(1, dom_count - 1, 2)]
    far_pairs = up + [(j, i) for i, j in up]
    sib_pairs = [(i, i ^ 1) for i in range(dom_count)]

    def far(v):
        return lax.ppermute(v, "dom", far_pairs)

    def near(v):
        return lax.ppermute(v, "dom", sib_pairs)

    def onward(v):
        return lax.ppermute(v, "segment", [(i, i + 1) for i in range(last)])

    def backward(v):
        return lax.ppermute(v, "segment", [(i + 1, i) for i in range(last)])

    part = functools.partial
    band, across = run(
        band_kernel,
        [((3, N, 3 * N), BF16), ((2, 3 * N, N), BF16)],
        adj_tiles,
        (tile_cols, pl.BlockSpec(memory_space=pltpu.SMEM)),
        scratch=[pltpu.VMEM((12, BLOCK, BLOCK), F32)],
        flops=PRODUCT,
    )
    gains, weights, turned = run(
        weight_kernel,
        [((2 * LAYERS, N), F32), ((3, 2 * LAYERS, N, N), BF16), ((2, 2 * LAYERS, N, N), BF16)],
        weight_first, weight_second, gain_first, gain_second, flops=PRODUCT,
    )
    out, cot, held = back_outputs[0], back_cotangents[0], forward_held[0]
    y1, y2, g1, g2 = half(out, 0), half(out, 1), half(cot, 0), half(cot, 1)
    x1, x2 = half(held, 0), half(held, 1)
    sent = run(
        part(entry_kernel, top_layer), [PACK], y1, g2, x2, across, gain_second, weight_second,
        gain_first, weight_first, flops=3 * PRODUCT,
    )[0]
    grads, results = {}, []
    for slot in range(2):
        for step in range(2 * LAYERS):
            even = step % 2 == 0
            l = top_layer - step // 2
            k = at(SECOND if even else FIRST, l)
            target, h, g, cot, x = (y2, y1, g2, g1, x1) if even else (y1, y2, g1, g2, x2)
            from_far = far(sent)
            inverse, owed, forward, sib, sib_owed = run(
                local_kernel, [MAT, MAT, MAT, PAIR, MAT], sent, target, g, x, band, across,
                flops=4 * PRODUCT,
            )
            from_near = (near(sib), near(sib_owed))
            inverse, owed, forward, xhat, rstd = run(
                near_kernel, [MAT, MAT, MAT, MAT, THIN], inverse, owed, forward, *from_near, h, band,
                flops=3 * PRODUCT,
            )
            operands = (inverse, owed, forward, from_far, xhat, rstd, cot, band, gains, turned)
            if step < 2 * LAYERS - 1:
                inverse_k = at(FIRST, l) if even else at(SECOND, l - 1)
                forward_k = at(SECOND, step // 2) if even else at(FIRST, step // 2 + 1)
                packed = [PAIR] if slot == 0 and step == 2 * LAYERS - 2 else []
                value, carried, ahead, back, sent, *packed = run(
                    part(join_kernel, k, inverse_k, forward_k), [MAT, MAT, MAT, MAT, PACK] + packed,
                    *operands, across, weights, flops=6 * PRODUCT,
                )
                if even:
                    y2, g1, x1 = value, carried, ahead
                else:
                    y1, g2, x2 = value, carried, ahead
                if packed:
                    early = backward(packed[0])
            elif slot == 0:
                *wholes, back, late, onwards = run(
                    part(last_kernel, False, k), [FULL, FULL, FULL, MAT, PAIR, PAIR], *operands, y2,
                    g1, x1, flops=4 * PRODUCT,
                )
                late, onwards = backward(late), onward(onwards)
            else:
                *wholes, keep, give = run(
                    part(last_kernel, True, k), [FULL, FULL, FULL, PAIR, PAIR], *operands, y2, g1,
                    x1, grads[at(FIRST, 0)], grads[at(FIRST, 1)], grads[at(SECOND, 0)],
                    grads[at(SECOND, 1)], flops=5 * PRODUCT,
                )
                break
            before = [grads[k]] if k in grads else []
            grads[k] = run(part(grad_kernel, k), [MAT], xhat, back, gains, *before, flops=PRODUCT)[0]
        results.append(wholes)
        if slot == 0:
            y1, y2, g1, g2, x1, x2, sent = run(
                part(next_kernel, at(SECOND, top_layer)), [MAT] * 6 + [PACK], back_new_outputs,
                back_new_cotangents, forward_new, early, late, onwards, across, gains, weights,
                flops=3 * PRODUCT,
            )

    groups = [list(range(c, dom_count, 2)) for c in range(2)]
    chips = dom_count // 2
    shares = (chips, LAYERS * N // chips, N)

    def exchanged(v):
        return lax.all_to_all(v, "dom", 0, 0, axis_index_groups=groups, tiled=True)

    summed = run(add_kernel, [PAIR], keep, near(give))[0]
    parts = exchanged(summed.reshape(shares))
    scale_factor = 1.0 / math.sqrt(2.0 * N * dom_count)
    mine = exchanged(run(part(share_kernel, scale_factor), [(shares, F32)], parts)[0])
    mine = mine.reshape(LAYERS * N, N)
    square, line = ((LAYERS, N, N), F32), ((LAYERS, N), F32)
    finals = run(
        finish_kernel, [square, square, line, line], mine, near(mine), weight_first, weight_second,
        gain_first, gain_second,
    )
    (inputs_a, cotan_a, ahead_a), (inputs_b, cotan_b, ahead_b) = results
    nodes = (ahead_a, ahead_b, inputs_a, cotan_a, inputs_b, cotan_b)
    return tuple(v[None] for v in nodes) + tuple(finals)


def solution(mesh):
    rows = P("segment", "dom", None)
    nodes = P("dom", None)
    weights = P("segment", None, None)
    gains = P("segment", None)
    return jax.shard_map(
        per_device,
        mesh=mesh,
        in_specs=(
            rows,
            nodes,
            rows,
            rows,
            nodes,
            nodes,
            P("dom", None, None, None),
            nodes,
            weights,
            weights,
            gains,
            gains,
        ),
        out_specs=(rows,) * 6 + (weights, weights, gains, gains),
        check_vma=False,
    )
```

```python
import functools
import math

import jax
import jax.numpy as jnp
from jax import lax
from jax.experimental import pallas as pl
from jax.experimental.pallas import tpu as pltpu
from jax.sharding import PartitionSpec as P

F32 = jnp.float32
BF16 = jnp.bfloat16
N = 256
BLOCK = 128
TILES = 16
LAYERS = 2
FIRST, SECOND = 0, 1
A, B, C = slice(0, N), slice(N, 2 * N), slice(2 * N, 3 * N)


def split(x):
    hi = x.astype(BF16)
    return hi, (x - hi.astype(F32)).astype(BF16)


def split3(x):
    hi = x.astype(BF16)
    rest = x - hi.astype(F32)
    mid = rest.astype(BF16)
    return hi, mid, (rest - mid.astype(F32)).astype(BF16)


def mm(a, b):
    return jnp.dot(a, b, preferred_element_type=F32)


def dot3(a, b):
    return mm(jnp.concatenate([a[0], a[0], a[1]], axis=1), jnp.concatenate([b[0], b[1], b[0]], axis=0))


def dot6(a, b):
    n = a[0].shape[0]
    p = mm(jnp.concatenate([a[0], a[1], a[2]], axis=0), b[0])
    q = mm(jnp.concatenate([a[0], a[1]], axis=0), b[1])
    small = mm(a[0], b[2]) + (p[2 * n :] + q[n:])
    return p[:n] + ((q[:n] + p[n : 2 * n]) + small)


def norm(h):
    centred = h - jnp.mean(h, axis=1, keepdims=True)
    rstd = lax.rsqrt(jnp.mean(centred * centred, axis=1, keepdims=True) + 1e-05)
    return centred * rstd, rstd


def active(h, gain):
    return jnp.maximum(norm(h)[0] * gain, 0.0)


def at(branch, l):
    return branch * LAYERS + l


def half(array, j):
    return array, pl.BlockSpec((N, N), lambda i: (0, j))


def run(kernel, outs, *operands, flops=0, scratch=()):
    arrays, specs = [], []
    for o in operands:
        pair = isinstance(o, tuple)
        arrays.append(o[0] if pair else o)
        specs.append(o[1] if pair else pl.BlockSpec(memory_space=pltpu.VMEM))
    return pl.pallas_call(
        kernel,
        out_shape=[jax.ShapeDtypeStruct(s, t) for s, t in outs],
        grid=(1,),
        in_specs=specs,
        out_specs=[pl.BlockSpec(memory_space=pltpu.VMEM)] * len(outs),
        scratch_shapes=list(scratch),
        compiler_params=pltpu.CompilerParams(vmem_limit_bytes=12 << 20),
        cost_estimate=pl.CostEstimate(flops=flops, bytes_accessed=1024, transcendentals=0),
    )(*arrays)


MAT = ((N, N), F32)
PAIR = ((2 * N, N), F32)
PACK = ((3 * N, N), F32)
FULL = ((N, 2 * N), F32)
THIN = ((N, BLOCK), F32)
PRODUCT = 1024


def band_kernel(tiles, cols, band, across, acc):
    dom = lax.axis_index("dom")
    parity = lax.rem(dom, 2)
    first = (dom - 1) * 2
    acc[...] = jnp.zeros_like(acc)
    for r in range(2):
        for t in range(TILES):
            place = cols[r, t] - first
            group = place // 2
            side = jnp.where(group == 2, 1, 0)
            which = jnp.where(group == 1, 0, jnp.where(side == parity, 2, 1))
            acc[r * 6 + which * 2 + (place - group * 2)] += tiles[r, t]
    for r in range(2):
        rows = slice(r * BLOCK, (r + 1) * BLOCK)
        for c in range(6):
            columns = slice(c * BLOCK, (c + 1) * BLOCK)
            block = acc[r * 6 + c]
            for i, piece in enumerate(split3(block)):
                band[i, rows, columns] = piece
            for i, piece in enumerate(split(block.T)):
                across[i, columns, rows] = piece


def weight_kernel(first, second, gain_first, gain_second, gains, weights, turned):
    for branch, (w, gain) in enumerate([(first, gain_first), (second, gain_second)]):
        for l in range(LAYERS):
            k = at(branch, l)
            gains[k : k + 1, :] = gain[l : l + 1, :]
            value = w[l]
            for i, piece in enumerate(split3(value)):
                weights[i, k] = piece
            for i, piece in enumerate(split(value.T)):
                turned[i, k] = piece


def pieces(ref, *where, count):
    return [ref[(i, *where)] for i in range(count)]


def mixed6(h, k, gains, weights):
    return dot6(split3(active(h, gains[k : k + 1, :])), pieces(weights, k, count=3))


def mixed3(h, k, gains, weights):
    return dot3(split(active(h, gains[k : k + 1, :])), pieces(weights, k, count=2))


def aggregate6(band, columns, values):
    return dot6(pieces(band, slice(0, N), columns, count=3), split3(values))


def aggregate3(band, columns, values):
    return dot3(pieces(band, slice(0, N), columns, count=2), split(values))


def owed_to(across, rows, g):
    return dot3(pieces(across, rows, slice(0, N), count=2), split(g))


def pulled(k, xhat, rstd, back, target, gains, turned):
    scale = gains[k : k + 1, :]
    grown = dot3(split(back), pieces(turned, k, count=2))
    dxhat = jnp.where(xhat * scale > 0.0, grown, 0.0) * scale
    inner = jnp.mean(dxhat * xhat, axis=1, keepdims=True)
    return target + rstd * (dxhat - jnp.mean(dxhat, axis=1, keepdims=True) - xhat * inner)


def weight_grad(k, xhat, back, gains):
    act = jnp.maximum(xhat * gains[k : k + 1, :], 0.0)
    return dot3(split(act.T), split(back))


def entry_kernel(l, y1, g2, x2, across, gain_second, weight_second, gain_first, weight_first, sent):
    act = active(y1[...], gain_second[l : l + 1, :])
    sent[A, :] = dot6(split3(act), split3(weight_second[l]))
    sent[B, :] = owed_to(across, C, g2[...])
    act = active(x2[...], gain_first[0:1, :])
    sent[C, :] = dot3(split(act), split(weight_first[0]))


def next_kernel(
    k, y_new, g_new, x_new, early, late, ahead, across, gains, weights,
    y1, y2, g1, g2, x1, x2, sent,
):
    segment = lax.axis_index("segment")
    is_last = segment == lax.axis_size("segment") - 1
    is_first = segment == 0
    upper = jnp.where(is_last, y_new[:, A], late[A, :])
    lower_cot = jnp.where(is_last, g_new[:, B], late[B, :])
    lower = jnp.where(is_first, x_new[:, B], ahead[B, :])
    sent[A, :] = mixed6(upper, k, gains, weights)
    sent[B, :] = owed_to(across, C, lower_cot)
    sent[C, :] = mixed3(lower, at(FIRST, 0), gains, weights)
    y1[...] = upper
    g2[...] = lower_cot
    x2[...] = lower
    y2[...] = jnp.where(is_last, y_new[:, B], early[A, :])
    g1[...] = jnp.where(is_last, g_new[:, A], early[B, :])
    x1[...] = jnp.where(is_first, x_new[:, A], ahead[A, :])


def local_kernel(sent, target, g, x, band, across, inverse, owed, forward, sib, sib_owed):
    mixed, fed = sent[A, :], sent[C, :]
    value = g[...]
    sib[A, :] = mixed
    sib[B, :] = fed
    sib_owed[...] = owed_to(across, B, value)
    owed[...] = owed_to(across, A, value)
    inverse[...] = target[...] - aggregate6(band, A, mixed)
    forward[...] = x[...] + aggregate3(band, A, fed)


def near_kernel(
    inverse, owed, forward, near, near_owed, h, band, inverse_out, owed_out, forward_out, xhat, rstd
):
    inverse_out[...] = inverse[...] - aggregate6(band, B, near[A, :])
    owed_out[...] = owed[...] + near_owed[...]
    forward_out[...] = forward[...] + aggregate3(band, B, near[B, :])
    normed, scale = norm(h[...])
    xhat[...] = normed
    rstd[...] = jnp.broadcast_to(scale, rstd.shape)


def joined(k, inverse, owed, forward, far, xhat, rstd, cot, band, gains, turned):
    value = inverse[...] - aggregate6(band, C, far[A, :])
    back = owed[...] + far[B, :]
    carried = pulled(k, xhat[...], rstd[:, 0:1], back, cot[...], gains, turned)
    ahead = forward[...] + aggregate3(band, C, far[C, :])
    return value, back, carried, ahead


def join_kernel(
    k, inverse_k, forward_k, inverse, owed, forward, far, xhat, rstd, cot, band, gains, turned,
    across, weights, value_out, carried_out, ahead_out, back_out, sent, *packed,
):
    value, back, carried, ahead = joined(
        k, inverse, owed, forward, far, xhat, rstd, cot, band, gains, turned
    )
    sent[A, :] = mixed6(value, inverse_k, gains, weights)
    sent[B, :] = owed_to(across, C, carried)
    sent[C, :] = mixed3(ahead, forward_k, gains, weights)
    value_out[...] = value
    carried_out[...] = carried
    ahead_out[...] = ahead
    back_out[...] = back
    if packed:
        packed[0][A, :] = value
        packed[0][B, :] = carried


def grad_kernel(k, xhat, back, gains, *refs):
    value = weight_grad(k, xhat[...], back[...], gains)
    refs[-1][...] = value + refs[0][...] if len(refs) > 1 else value


def final_grad_kernel(
    k, owed, far, xhat, gains, before, first_high, second_low, second_high, keep, give
):
    grad = before[...] + weight_grad(k, xhat[...], owed[...] + far[B, :], gains)
    even = lax.rem(lax.axis_index("dom"), 2) == 0
    keep[A, :] = jnp.where(even, grad, second_low[...])
    keep[B, :] = jnp.where(even, first_high[...], second_high[...])
    give[A, :] = jnp.where(even, second_low[...], grad)
    give[B, :] = jnp.where(even, second_high[...], first_high[...])


def last_kernel(
    final, k, inverse, owed, forward, far, xhat, rstd, cot, band, gains, turned, low, top_cot, top,
    whole, whole_cot, whole_ahead, *refs,
):
    value, back, carried, ahead = joined(
        k, inverse, owed, forward, far, xhat, rstd, cot, band, gains, turned
    )
    whole[:, A] = value
    whole[:, B] = low[...]
    whole_cot[:, A] = top_cot[...]
    whole_cot[:, B] = carried
    whole_ahead[:, A] = top[...]
    whole_ahead[:, B] = ahead
    if not final:
        back_out, late, ahead_out = refs
        back_out[...] = back
        late[A, :] = value
        late[B, :] = carried
        ahead_out[A, :] = top[...]
        ahead_out[B, :] = ahead


def add_kernel(a, b, out):
    out[...] = a[...] + b[...]


def share_kernel(scale, parts, out):
    total = jnp.sum(parts[...], axis=0) * scale
    out[...] = jnp.broadcast_to(total[None], out.shape)


def finish_kernel(
    mine, theirs, weight_first, weight_second, gain_first, gain_second, first, second, dgf, dgs
):
    even = lax.rem(lax.axis_index("dom"), 2) == 0
    a = mine[...]
    b = theirs[...]
    wf = jnp.where(even, a, b).reshape(first.shape)
    ws = jnp.where(even, b, a).reshape(second.shape)
    first[...] = wf
    second[...] = ws
    dgf[...] = jnp.sum(wf * weight_first[...], axis=2) / gain_first[...]
    dgs[...] = jnp.sum(ws * weight_second[...], axis=2) / gain_second[...]


def per_device(
    forward_held,
    forward_new,
    back_outputs,
    back_cotangents,
    back_new_outputs,
    back_new_cotangents,
    adj_tiles,
    tile_cols,
    weight_first,
    weight_second,
    gain_first,
    gain_second,
):
    dom_count = lax.axis_size("dom")
    last = lax.axis_size("segment") - 1
    top_layer = LAYERS - 1
    up = [(i, i + 1) for i in range(1, dom_count - 1, 2)]
    far_pairs = up + [(j, i) for i, j in up]
    sib_pairs = [(i, i ^ 1) for i in range(dom_count)]

    def far(v):
        return lax.ppermute(v, "dom", far_pairs)

    def near(v):
        return lax.ppermute(v, "dom", sib_pairs)

    def onward(v):
        return lax.ppermute(v, "segment", [(i, i + 1) for i in range(last)])

    def backward(v):
        return lax.ppermute(v, "segment", [(i + 1, i) for i in range(last)])

    part = functools.partial
    band, across = run(
        band_kernel,
        [((3, N, 3 * N), BF16), ((2, 3 * N, N), BF16)],
        adj_tiles,
        (tile_cols, pl.BlockSpec(memory_space=pltpu.SMEM)),
        scratch=[pltpu.VMEM((12, BLOCK, BLOCK), F32)],
        flops=PRODUCT,
    )
    gains, weights, turned = run(
        weight_kernel,
        [((2 * LAYERS, N), F32), ((3, 2 * LAYERS, N, N), BF16), ((2, 2 * LAYERS, N, N), BF16)],
        weight_first, weight_second, gain_first, gain_second, flops=PRODUCT,
    )
    out, cot, held = back_outputs[0], back_cotangents[0], forward_held[0]
    y1, y2, g1, g2 = half(out, 0), half(out, 1), half(cot, 0), half(cot, 1)
    x1, x2 = half(held, 0), half(held, 1)
    sent = run(
        part(entry_kernel, top_layer), [PACK], y1, g2, x2, across, gain_second, weight_second,
        gain_first, weight_first, flops=3 * PRODUCT,
    )[0]
    grads, results = {}, []
    for slot in range(2):
        for step in range(2 * LAYERS):
            even = step % 2 == 0
            l = top_layer - step // 2
            k = at(SECOND if even else FIRST, l)
            target, h, g, cot, x = (y2, y1, g2, g1, x1) if even else (y1, y2, g1, g2, x2)
            from_far = far(sent)
            inverse, owed, forward, sib, sib_owed = run(
                local_kernel, [MAT, MAT, MAT, PAIR, MAT], sent, target, g, x, band, across,
                flops=4 * PRODUCT,
            )
            from_near = (near(sib), near(sib_owed))
            inverse, owed, forward, xhat, rstd = run(
                near_kernel, [MAT, MAT, MAT, MAT, THIN], inverse, owed, forward, *from_near, h, band,
                flops=3 * PRODUCT,
            )
            operands = (inverse, owed, forward, from_far, xhat, rstd, cot, band, gains, turned)
            if step < 2 * LAYERS - 1:
                inverse_k = at(FIRST, l) if even else at(SECOND, l - 1)
                forward_k = at(SECOND, step // 2) if even else at(FIRST, step // 2 + 1)
                packed = [PAIR] if slot == 0 and step == 2 * LAYERS - 2 else []
                value, carried, ahead, back, sent, *packed = run(
                    part(join_kernel, k, inverse_k, forward_k), [MAT, MAT, MAT, MAT, PACK] + packed,
                    *operands, across, weights, flops=6 * PRODUCT,
                )
                if even:
                    y2, g1, x1 = value, carried, ahead
                else:
                    y1, g2, x2 = value, carried, ahead
                if packed:
                    early = backward(packed[0])
            elif slot == 0:
                *wholes, back, late, onwards = run(
                    part(last_kernel, False, k), [FULL, FULL, FULL, MAT, PAIR, PAIR], *operands, y2,
                    g1, x1, flops=4 * PRODUCT,
                )
                late, onwards = backward(late), onward(onwards)
            else:
                keep, give = run(
                    part(final_grad_kernel, k), [PAIR, PAIR], owed, from_far, xhat, gains,
                    grads[at(FIRST, 0)], grads[at(FIRST, 1)], grads[at(SECOND, 0)],
                    grads[at(SECOND, 1)], flops=PRODUCT,
                )
                wholes = run(
                    part(last_kernel, True, k), [FULL, FULL, FULL], *operands, y2, g1, x1,
                    flops=5 * PRODUCT,
                )
                break
            before = [grads[k]] if k in grads else []
            grads[k] = run(part(grad_kernel, k), [MAT], xhat, back, gains, *before, flops=PRODUCT)[0]
        results.append(wholes)
        if slot == 0:
            y1, y2, g1, g2, x1, x2, sent = run(
                part(next_kernel, at(SECOND, top_layer)), [MAT] * 6 + [PACK], back_new_outputs,
                back_new_cotangents, forward_new, early, late, onwards, across, gains, weights,
                flops=3 * PRODUCT,
            )

    groups = [list(range(c, dom_count, 2)) for c in range(2)]
    chips = dom_count // 2
    shares = (chips, LAYERS * N // chips, N)

    def exchanged(v):
        return lax.all_to_all(v, "dom", 0, 0, axis_index_groups=groups, tiled=True)

    summed = run(add_kernel, [PAIR], keep, near(give))[0]
    parts = exchanged(summed.reshape(shares))
    scale_factor = 1.0 / math.sqrt(2.0 * N * dom_count)
    mine = exchanged(run(part(share_kernel, scale_factor), [(shares, F32)], parts)[0])
    mine = mine.reshape(LAYERS * N, N)
    square, line = ((LAYERS, N, N), F32), ((LAYERS, N), F32)
    finals = run(
        finish_kernel, [square, square, line, line], mine, near(mine), weight_first, weight_second,
        gain_first, gain_second,
    )
    (inputs_a, cotan_a, ahead_a), (inputs_b, cotan_b, ahead_b) = results
    nodes = (ahead_a, ahead_b, inputs_a, cotan_a, inputs_b, cotan_b)
    return tuple(v[None] for v in nodes) + tuple(finals)


def solution(mesh):
    rows = P("segment", "dom", None)
    nodes = P("dom", None)
    weights = P("segment", None, None)
    gains = P("segment", None)
    return jax.shard_map(
        per_device,
        mesh=mesh,
        in_specs=(
            rows,
            nodes,
            rows,
            rows,
            nodes,
            nodes,
            P("dom", None, None, None),
            nodes,
            weights,
            weights,
            gains,
            gains,
        ),
        out_specs=(rows,) * 6 + (weights, weights, gains, gains),
        check_vma=False,
    )
```

```python
import functools
import math

import jax
import jax.numpy as jnp
from jax import lax
from jax.experimental import pallas as pl
from jax.experimental.pallas import tpu as pltpu
from jax.sharding import PartitionSpec as P

F32 = jnp.float32
BF16 = jnp.bfloat16
N = 256
BLOCK = 128
TILES = 16
LAYERS = 2
FIRST, SECOND = 0, 1
A, B, C = slice(0, N), slice(N, 2 * N), slice(2 * N, 3 * N)


def split(x):
    hi = x.astype(BF16)
    return hi, (x - hi.astype(F32)).astype(BF16)


def split3(x):
    hi = x.astype(BF16)
    rest = x - hi.astype(F32)
    mid = rest.astype(BF16)
    return hi, mid, (rest - mid.astype(F32)).astype(BF16)


def mm(a, b):
    return jnp.dot(a, b, preferred_element_type=F32)


def dot3(a, b):
    return mm(jnp.concatenate([a[0], a[0], a[1]], axis=1), jnp.concatenate([b[0], b[1], b[0]], axis=0))


def dot6(a, b):
    n = a[0].shape[0]
    p = mm(jnp.concatenate([a[0], a[1], a[2]], axis=0), b[0])
    q = mm(jnp.concatenate([a[0], a[1]], axis=0), b[1])
    small = mm(a[0], b[2]) + (p[2 * n :] + q[n:])
    return p[:n] + ((q[:n] + p[n : 2 * n]) + small)


def norm(h):
    centred = h - jnp.mean(h, axis=1, keepdims=True)
    rstd = lax.rsqrt(jnp.mean(centred * centred, axis=1, keepdims=True) + 1e-05)
    return centred * rstd, rstd


def active(h, gain):
    return jnp.maximum(norm(h)[0] * gain, 0.0)


def at(branch, l):
    return branch * LAYERS + l


def half(array, j):
    return array, pl.BlockSpec((N, N), lambda i: (0, j))


def run(kernel, outs, *operands, flops=0, scratch=(), limit=12):
    arrays, specs = [], []
    for o in operands:
        pair = isinstance(o, tuple)
        arrays.append(o[0] if pair else o)
        specs.append(o[1] if pair else pl.BlockSpec(memory_space=pltpu.VMEM))
    return pl.pallas_call(
        kernel,
        out_shape=[jax.ShapeDtypeStruct(s, t) for s, t in outs],
        grid=(1,),
        in_specs=specs,
        out_specs=[pl.BlockSpec(memory_space=pltpu.VMEM)] * len(outs),
        scratch_shapes=list(scratch),
        compiler_params=pltpu.CompilerParams(vmem_limit_bytes=limit << 20),
        cost_estimate=pl.CostEstimate(flops=flops, bytes_accessed=1024, transcendentals=0),
    )(*arrays)


MAT = ((N, N), F32)
PAIR = ((2 * N, N), F32)
PACK = ((3 * N, N), F32)
FULL = ((N, 2 * N), F32)
THIN = ((N, BLOCK), F32)
PRODUCT = 1024


def first_kernel(
    l, tiles_at, cols_at, y_at, g_at, x_at, gain_second, weight_second_at, gain_first,
    weight_first_at, band, across, sent, acc, tiles, cols, values, sems,
):
    copies = [
        pltpu.make_async_copy(source, target, sems.at[i])
        for i, (source, target) in enumerate(
            [
                (weight_second_at.at[l], values.at[0]),
                (y_at.at[:, pl.ds(0, N)], values.at[1]),
                (weight_first_at.at[0], values.at[2]),
                (x_at.at[:, pl.ds(N, N)], values.at[3]),
                (g_at.at[:, pl.ds(N, N)], values.at[4]),
                (cols_at, cols),
                (tiles_at, tiles),
            ]
        )
    ]
    for copy in copies:
        copy.start()
    acc[...] = jnp.zeros_like(acc)
    for copy in copies[:4]:
        copy.wait()
    act = active(values[1], gain_second[l : l + 1, :])
    sent[A, :] = dot6(split3(act), split3(values[0]))
    act = active(values[3], gain_first[0:1, :])
    sent[C, :] = dot3(split(act), split(values[2]))
    for copy in copies[4:]:
        copy.wait()
    dom = lax.axis_index("dom")
    parity = lax.rem(dom, 2)
    first = (dom - 1) * 2
    for r in range(2):
        for t in range(TILES):
            place = cols[r, t] - first
            group = place // 2
            side = jnp.where(group == 2, 1, 0)
            which = jnp.where(group == 1, 0, jnp.where(side == parity, 2, 1))
            acc[r * 6 + which * 2 + (place - group * 2)] += tiles[r, t]
    for r in range(2):
        rows = slice(r * BLOCK, (r + 1) * BLOCK)
        for c in range(6):
            columns = slice(c * BLOCK, (c + 1) * BLOCK)
            block = acc[r * 6 + c]
            for i, piece in enumerate(split3(block)):
                band[i, rows, columns] = piece
            for i, piece in enumerate(split(block.T)):
                across[i, columns, rows] = piece
    sent[B, :] = owed_to(across, C, values[4])


def weight_kernel(first, second, gain_first, gain_second, gains, weights, turned):
    for branch, (w, gain) in enumerate([(first, gain_first), (second, gain_second)]):
        for l in range(LAYERS):
            k = at(branch, l)
            gains[k : k + 1, :] = gain[l : l + 1, :]
            value = w[l]
            for i, piece in enumerate(split3(value)):
                weights[i, k] = piece
            for i, piece in enumerate(split(value.T)):
                turned[i, k] = piece


def pieces(ref, *where, count):
    return [ref[(i, *where)] for i in range(count)]


def mixed6(h, k, gains, weights):
    return dot6(split3(active(h, gains[k : k + 1, :])), pieces(weights, k, count=3))


def mixed3(h, k, gains, weights):
    return dot3(split(active(h, gains[k : k + 1, :])), pieces(weights, k, count=2))


def aggregate6(band, columns, values):
    return dot6(pieces(band, slice(0, N), columns, count=3), split3(values))


def aggregate3(band, columns, values):
    return dot3(pieces(band, slice(0, N), columns, count=2), split(values))


def owed_to(across, rows, g):
    return dot3(pieces(across, rows, slice(0, N), count=2), split(g))


def pulled(k, xhat, rstd, back, target, gains, turned):
    scale = gains[k : k + 1, :]
    grown = dot3(split(back), pieces(turned, k, count=2))
    dxhat = jnp.where(xhat * scale > 0.0, grown, 0.0) * scale
    inner = jnp.mean(dxhat * xhat, axis=1, keepdims=True)
    return target + rstd * (dxhat - jnp.mean(dxhat, axis=1, keepdims=True) - xhat * inner)


def weight_grad(k, xhat, back, gains):
    act = jnp.maximum(xhat * gains[k : k + 1, :], 0.0)
    return dot3(split(act.T), split(back))


def next_kernel(
    k, y_new, g_new, x_new, early, late, ahead, across, gains, weights,
    y1, y2, g1, g2, x1, x2, sent,
):
    segment = lax.axis_index("segment")
    is_last = segment == lax.axis_size("segment") - 1
    is_first = segment == 0
    upper = jnp.where(is_last, y_new[:, A], late[A, :])
    lower_cot = jnp.where(is_last, g_new[:, B], late[B, :])
    lower = jnp.where(is_first, x_new[:, B], ahead[B, :])
    sent[A, :] = mixed6(upper, k, gains, weights)
    sent[B, :] = owed_to(across, C, lower_cot)
    sent[C, :] = mixed3(lower, at(FIRST, 0), gains, weights)
    y1[...] = upper
    g2[...] = lower_cot
    x2[...] = lower
    y2[...] = jnp.where(is_last, y_new[:, B], early[A, :])
    g1[...] = jnp.where(is_last, g_new[:, A], early[B, :])
    x1[...] = jnp.where(is_first, x_new[:, A], ahead[A, :])


def local_kernel(sent, target, g, x, band, across, inverse, owed, forward, sib, sib_owed):
    mixed, fed = sent[A, :], sent[C, :]
    value = g[...]
    sib[A, :] = mixed
    sib[B, :] = fed
    sib_owed[...] = owed_to(across, B, value)
    owed[...] = owed_to(across, A, value)
    inverse[...] = target[...] - aggregate6(band, A, mixed)
    forward[...] = x[...] + aggregate3(band, A, fed)


def near_kernel(
    inverse, owed, forward, near, near_owed, h, band, inverse_out, owed_out, forward_out, xhat, rstd
):
    inverse_out[...] = inverse[...] - aggregate6(band, B, near[A, :])
    owed_out[...] = owed[...] + near_owed[...]
    forward_out[...] = forward[...] + aggregate3(band, B, near[B, :])
    normed, scale = norm(h[...])
    xhat[...] = normed
    rstd[...] = jnp.broadcast_to(scale, rstd.shape)


def joined(k, inverse, owed, forward, far, xhat, rstd, cot, band, gains, turned):
    value = inverse[...] - aggregate6(band, C, far[A, :])
    back = owed[...] + far[B, :]
    carried = pulled(k, xhat[...], rstd[:, 0:1], back, cot[...], gains, turned)
    ahead = forward[...] + aggregate3(band, C, far[C, :])
    return value, back, carried, ahead


def join_kernel(
    k, inverse_k, forward_k, inverse, owed, forward, far, xhat, rstd, cot, band, gains, turned,
    across, weights, value_out, carried_out, ahead_out, back_out, sent, *packed,
):
    value, back, carried, ahead = joined(
        k, inverse, owed, forward, far, xhat, rstd, cot, band, gains, turned
    )
    sent[A, :] = mixed6(value, inverse_k, gains, weights)
    sent[B, :] = owed_to(across, C, carried)
    sent[C, :] = mixed3(ahead, forward_k, gains, weights)
    value_out[...] = value
    carried_out[...] = carried
    ahead_out[...] = ahead
    back_out[...] = back
    if packed:
        packed[0][A, :] = value
        packed[0][B, :] = carried


def grad_kernel(k, xhat, back, gains, *refs):
    value = weight_grad(k, xhat[...], back[...], gains)
    refs[-1][...] = value + refs[0][...] if len(refs) > 1 else value


def final_grad_kernel(
    k, owed, far, xhat, gains, before, first_high, second_low, second_high, keep, give
):
    grad = before[...] + weight_grad(k, xhat[...], owed[...] + far[B, :], gains)
    even = lax.rem(lax.axis_index("dom"), 2) == 0
    keep[A, :] = jnp.where(even, grad, second_low[...])
    keep[B, :] = jnp.where(even, first_high[...], second_high[...])
    give[A, :] = jnp.where(even, second_low[...], grad)
    give[B, :] = jnp.where(even, second_high[...], first_high[...])


def last_kernel(
    final, k, inverse, owed, forward, far, xhat, rstd, cot, band, gains, turned, low, top_cot, top,
    whole, whole_cot, whole_ahead, *refs,
):
    value, back, carried, ahead = joined(
        k, inverse, owed, forward, far, xhat, rstd, cot, band, gains, turned
    )
    whole[:, A] = value
    whole[:, B] = low[...]
    whole_cot[:, A] = top_cot[...]
    whole_cot[:, B] = carried
    whole_ahead[:, A] = top[...]
    whole_ahead[:, B] = ahead
    if not final:
        back_out, late, ahead_out = refs
        back_out[...] = back
        late[A, :] = value
        late[B, :] = carried
        ahead_out[A, :] = top[...]
        ahead_out[B, :] = ahead


def add_kernel(a, b, out):
    out[...] = a[...] + b[...]


def share_kernel(scale, parts, out):
    total = jnp.sum(parts[...], axis=0) * scale
    out[...] = jnp.broadcast_to(total[None], out.shape)


def finish_kernel(
    mine, theirs, weight_first, weight_second, gain_first, gain_second, first, second, dgf, dgs
):
    even = lax.rem(lax.axis_index("dom"), 2) == 0
    a = mine[...]
    b = theirs[...]
    wf = jnp.where(even, a, b).reshape(first.shape)
    ws = jnp.where(even, b, a).reshape(second.shape)
    first[...] = wf
    second[...] = ws
    dgf[...] = jnp.sum(wf * weight_first[...], axis=2) / gain_first[...]
    dgs[...] = jnp.sum(ws * weight_second[...], axis=2) / gain_second[...]


def per_device(
    forward_held,
    forward_new,
    back_outputs,
    back_cotangents,
    back_new_outputs,
    back_new_cotangents,
    adj_tiles,
    tile_cols,
    weight_first,
    weight_second,
    gain_first,
    gain_second,
):
    dom_count = lax.axis_size("dom")
    last = lax.axis_size("segment") - 1
    top_layer = LAYERS - 1
    up = [(i, i + 1) for i in range(1, dom_count - 1, 2)]
    far_pairs = up + [(j, i) for i, j in up]
    sib_pairs = [(i, i ^ 1) for i in range(dom_count)]

    def far(v):
        return lax.ppermute(v, "dom", far_pairs)

    def near(v):
        return lax.ppermute(v, "dom", sib_pairs)

    def onward(v):
        return lax.ppermute(v, "segment", [(i, i + 1) for i in range(last)])

    def backward(v):
        return lax.ppermute(v, "segment", [(i + 1, i) for i in range(last)])

    part = functools.partial
    gains, weights, turned = run(
        weight_kernel,
        [((2 * LAYERS, N), F32), ((3, 2 * LAYERS, N, N), BF16), ((2, 2 * LAYERS, N, N), BF16)],
        weight_first, weight_second, gain_first, gain_second, flops=PRODUCT,
    )
    out, cot, held = back_outputs[0], back_cotangents[0], forward_held[0]
    y1, y2, g1, g2 = half(out, 0), half(out, 1), half(cot, 0), half(cot, 1)
    x1, x2 = half(held, 0), half(held, 1)
    hbm = pl.BlockSpec(memory_space=pl.ANY)
    band, across, sent = run(
        part(first_kernel, top_layer),
        [((3, N, 3 * N), BF16), ((2, 3 * N, N), BF16), PACK],
        (adj_tiles, hbm), (tile_cols, hbm), (out, hbm), (cot, hbm), (held, hbm), gain_second,
        (weight_second, hbm), gain_first, (weight_first, hbm),
        scratch=[
            pltpu.VMEM((12, BLOCK, BLOCK), F32),
            pltpu.VMEM((2, TILES, BLOCK, BLOCK), F32),
            pltpu.SMEM((2, TILES), jnp.int32),
            pltpu.VMEM((5, N, N), F32),
            pltpu.SemaphoreType.DMA((7,)),
        ],
        flops=PRODUCT,
        limit=54,
    )
    grads, results = {}, []
    for slot in range(2):
        for step in range(2 * LAYERS):
            even = step % 2 == 0
            l = top_layer - step // 2
            k = at(SECOND if even else FIRST, l)
            target, h, g, cot, x = (y2, y1, g2, g1, x1) if even else (y1, y2, g1, g2, x2)
            from_far = far(sent)
            inverse, owed, forward, sib, sib_owed = run(
                local_kernel, [MAT, MAT, MAT, PAIR, MAT], sent, target, g, x, band, across,
                flops=4 * PRODUCT,
            )
            from_near = (near(sib), near(sib_owed))
            inverse, owed, forward, xhat, rstd = run(
                near_kernel, [MAT, MAT, MAT, MAT, THIN], inverse, owed, forward, *from_near, h, band,
                flops=3 * PRODUCT,
            )
            operands = (inverse, owed, forward, from_far, xhat, rstd, cot, band, gains, turned)
            if step < 2 * LAYERS - 1:
                inverse_k = at(FIRST, l) if even else at(SECOND, l - 1)
                forward_k = at(SECOND, step // 2) if even else at(FIRST, step // 2 + 1)
                packed = [PAIR] if slot == 0 and step == 2 * LAYERS - 2 else []
                value, carried, ahead, back, sent, *packed = run(
                    part(join_kernel, k, inverse_k, forward_k), [MAT, MAT, MAT, MAT, PACK] + packed,
                    *operands, across, weights, flops=6 * PRODUCT,
                )
                if even:
                    y2, g1, x1 = value, carried, ahead
                else:
                    y1, g2, x2 = value, carried, ahead
                if packed:
                    early = backward(packed[0])
            elif slot == 0:
                *wholes, back, late, onwards = run(
                    part(last_kernel, False, k), [FULL, FULL, FULL, MAT, PAIR, PAIR], *operands, y2,
                    g1, x1, flops=4 * PRODUCT,
                )
                late, onwards = backward(late), onward(onwards)
            else:
                keep, give = run(
                    part(final_grad_kernel, k), [PAIR, PAIR], owed, from_far, xhat, gains,
                    grads[at(FIRST, 0)], grads[at(FIRST, 1)], grads[at(SECOND, 0)],
                    grads[at(SECOND, 1)], flops=PRODUCT,
                )
                wholes = run(
                    part(last_kernel, True, k), [FULL, FULL, FULL], *operands, y2, g1, x1,
                    flops=5 * PRODUCT,
                )
                break
            before = [grads[k]] if k in grads else []
            grads[k] = run(part(grad_kernel, k), [MAT], xhat, back, gains, *before, flops=PRODUCT)[0]
        results.append(wholes)
        if slot == 0:
            y1, y2, g1, g2, x1, x2, sent = run(
                part(next_kernel, at(SECOND, top_layer)), [MAT] * 6 + [PACK], back_new_outputs,
                back_new_cotangents, forward_new, early, late, onwards, across, gains, weights,
                flops=3 * PRODUCT,
            )

    groups = [list(range(c, dom_count, 2)) for c in range(2)]
    chips = dom_count // 2
    shares = (chips, LAYERS * N // chips, N)

    def exchanged(v):
        return lax.all_to_all(v, "dom", 0, 0, axis_index_groups=groups, tiled=True)

    summed = run(add_kernel, [PAIR], keep, near(give))[0]
    parts = exchanged(summed.reshape(shares))
    scale_factor = 1.0 / math.sqrt(2.0 * N * dom_count)
    mine = exchanged(run(part(share_kernel, scale_factor), [(shares, F32)], parts)[0])
    mine = mine.reshape(LAYERS * N, N)
    square, line = ((LAYERS, N, N), F32), ((LAYERS, N), F32)
    finals = run(
        finish_kernel, [square, square, line, line], mine, near(mine), weight_first, weight_second,
        gain_first, gain_second,
    )
    (inputs_a, cotan_a, ahead_a), (inputs_b, cotan_b, ahead_b) = results
    nodes = (ahead_a, ahead_b, inputs_a, cotan_a, inputs_b, cotan_b)
    return tuple(v[None] for v in nodes) + tuple(finals)


def solution(mesh):
    rows = P("segment", "dom", None)
    nodes = P("dom", None)
    weights = P("segment", None, None)
    gains = P("segment", None)
    return jax.shard_map(
        per_device,
        mesh=mesh,
        in_specs=(
            rows,
            nodes,
            rows,
            rows,
            nodes,
            nodes,
            P("dom", None, None, None),
            nodes,
            weights,
            weights,
            gains,
            gains,
        ),
        out_specs=(rows,) * 6 + (weights, weights, gains, gains),
        check_vma=False,
    )
```
